512 devices in a mesh: frame: 16 (over x, y), head: 16 (over z), tok: 2 (over core).
Axes of the slice: x: 4, y: 4, z: 16, core: 2. Of those that a mesh axis runs over, the one named last changes fastest.
Arguments:
- queries: bfloat16 [16, 3072, 2048], P('frame', ('head', 'tok')), may hold values from -120 to 120
- keys: bfloat16 [16, 3072, 2048], P('frame', ('head', 'tok')), may hold values from -4 to 4
- values: bfloat16 [16, 3072, 2048], P('frame', ('head', 'tok')), may hold values from -6 to 6
- residual: bfloat16 [16, 3072, 2048], P('frame', ('head', 'tok')), may hold values from -6 to 6
- incoming: bfloat16 [3072, 2048], P(('head', 'tok')), may hold values from -6 to 6
- gate_table: float32 [50, 2048], replicated, may hold values from -2 to 2
- timesteps: int32 [16], P('frame'), may hold values from 0 to 49
- positions: int32 [16], P('frame'), may hold values from 0 to 45, as said below
Outputs:
- next_queue: bfloat16 [16, 3072, 2048], P('frame', ('head', 'tok'))
- leaving: bfloat16 [3072, 2048], P(('head', 'tok'), 'frame')
The draws below stay inside these ranges and needn't reach their ends.
Inputs may be any that keep to these rules, and one draw needn't show every extreme that they name: positions rise strictly along the queue, by 1 to 5 from one frame to the next; the first frame's position is 0 and the last frame's is 45.
All inputs are finite; a program needn't handle non-finite values.
Results may differ from the reference program's by a relative error of at most 0.007.
Values may be sent and summed in bfloat16 or wider, within the bound.
No kernel may reach another device: no remote copies, remote signals or barrier semaphores. Data moves between devices by JAX's collectives and lax.ppermute only.
A program may use at most 64 MiB of HBM per device.

```python
import math
import jax
import jax.numpy as jnp
from jax import lax

HD = 128
HEADS = 16
HH = 2048
FRAME_TOK = 3072
FRAMES = 16
STEPS = 50
ROPE_DIMS = 16


def drawn_base(key):
    array_shape = (FRAMES, FRAME_TOK, HEADS * HD)
    base_keys = jnp.clip(jax.random.normal(jax.random.fold_in(key, 101), array_shape, jnp.float32), -4.0, 4.0)
    return base_keys


def draw_keys(key, part):
    base_keys = drawn_base(key)
    return base_keys.astype(jnp.bfloat16)


def draw_queries(key, part):
    base_keys = drawn_base(key)
    key = jax.random.fold_in(key, 4)
    spread = 2.5 * jnp.clip(jax.random.normal(jax.random.fold_in(key, 1), base_keys.shape, jnp.float32), -4.0, 4.0)
    return spread.astype(jnp.bfloat16)


def draw_positions(key, part):
    key = jax.random.fold_in(key, 5)
    jitter = jax.random.randint(jax.random.fold_in(key, 1), (FRAMES,), 0, 3)
    frame_ids = jnp.arange(FRAMES, dtype=jnp.int32)
    pinned = (frame_ids == 0) | (frame_ids == FRAMES - 1)
    jitter = jnp.where(pinned, 0, jitter)
    return (3 * frame_ids + jitter).astype(jnp.int32)


def with_ends(entries, stream_key, smallest, high):
    longest = entries.shape.index(max(entries.shape))
    spots = []
    for shift in (0, 1):
        where = [jax.random.randint(jax.random.fold_in(stream_key, axis), (), 0, length) for axis, length in enumerate(entries.shape)]
        where[longest] = (where[longest] + shift) % entries.shape[longest]
        spots.append(tuple(where))
    return entries.at[spots[0]].set(smallest).at[spots[1]].set(high)


def level_of(own_key, shape, shards, low, largest):
    loudness, own = 1.0, jax.random.fold_in(own_key, 6)
    for position, shards_of in shards:
        steps = jnp.exp(jax.random.uniform(jax.random.fold_in(own, position), (shards_of,), jnp.float32, low / len(shards), largest / len(shards)))
        loudness = loudness * jnp.repeat(steps, shape[position] // shards_of).reshape([-1 if axis == position else 1 for axis in range(len(shape))])
    return loudness


def centred(own_key, extent, scale, most, split=(), kind=jnp.bfloat16):
    gain = level_of(own_key, extent, split, -0.22, 0.18) if split else 1.0
    result = jax.random.normal(own_key, extent, jnp.float32) * scale * gain
    return jnp.minimum(jnp.maximum(result, -most), most).astype(kind)


def setup_inputs(seed: int = 0) -> dict:
    arg_keys = jax.random.split(jax.random.key(seed), 9)
    return {
        "queries": draw_queries(jax.random.fold_in(arg_keys[8], 71), 0),
        "keys": draw_keys(jax.random.fold_in(arg_keys[8], 71), 0),
        "values": centred(arg_keys[2], (FRAMES, FRAME_TOK, HH), 1.0, 6.0, ((0, 16), (1, 32))),
        "residual": centred(arg_keys[3], (FRAMES, FRAME_TOK, HH), 1.0, 6.0, ((0, 16), (1, 32))),
        "incoming": centred(arg_keys[4], (FRAME_TOK, HH), 1.0, 6.0, ((0, 32),)),
        "gate_table": jnp.clip(jax.random.uniform(arg_keys[5], (STEPS, HH), jnp.float32, -2.0, 2.0), -2.0, 2.0),
        "timesteps": with_ends(jax.random.randint(arg_keys[6], (FRAMES,), 0, STEPS), jax.random.fold_in(arg_keys[6], 1), 0, STEPS - 1).astype(jnp.int32),
        "positions": draw_positions(jax.random.fold_in(arg_keys[8], 71), 0),
    }


rope_base = 256.0

def rotate(block_data, positions):
    frames, tokens, columns_all = block_data.shape
    shaped = block_data.astype(jnp.float32).reshape(frames, tokens, columns_all // HD, HD)
    half_dims = ROPE_DIMS // 2
    frequency = rope_base ** (-jnp.arange(half_dims, dtype=jnp.float32) / half_dims)
    angles = positions.astype(jnp.float32)[:, None, None, None] * frequency
    cosine = jnp.cos(angles)
    sine_term = jnp.sin(angles)
    leading = shaped[..., :half_dims]
    second = shaped[..., half_dims:ROPE_DIMS]
    turned = jnp.concatenate([leading * cosine - second * sine_term, second * cosine + leading * sine_term, shaped[..., ROPE_DIMS:]], axis=-1)
    return turned.reshape(frames, tokens, columns_all).astype(jnp.bfloat16)

def reference(queries, keys, values, residual, incoming, gate_table, timesteps, positions):
    turned_queries = rotate(queries, positions)
    turned_keys = rotate(keys, positions)
    score_scale = 1.0 / math.sqrt(HD)
    offsets = jnp.array([-1, 0, 1], dtype=jnp.int32)

    def one_frame(frame_index):
        nearby = frame_index + offsets
        usable = (nearby >= 0) & (nearby < FRAMES)
        picked = jnp.clip(nearby, 0, FRAMES - 1).astype(jnp.int32)
        near_keys = jnp.take(turned_keys, picked, axis=0).reshape(3 * FRAME_TOK, HH)
        near_values = jnp.take(values, picked, axis=0).reshape(3 * FRAME_TOK, HH)
        key_mask = jnp.repeat(usable, FRAME_TOK)
        own_queries = lax.dynamic_index_in_dim(turned_queries, frame_index, 0, keepdims=False)

        def one_head(head_index):
            start_col = (head_index * HD).astype(jnp.int32)
            head_queries = lax.dynamic_slice_in_dim(own_queries, start_col, HD, 1)
            head_keys = lax.dynamic_slice_in_dim(near_keys, start_col, HD, 1)
            head_values = lax.dynamic_slice_in_dim(near_values, start_col, HD, 1)
            scores = jnp.dot(head_queries, head_keys.T, preferred_element_type=jnp.float32) * score_scale
            scores = jnp.where(key_mask[None, :], scores, -jnp.inf)
            highest = lax.optimization_barrier(jnp.max(scores, axis=1, keepdims=True))
            weights = jnp.exp(scores - highest)
            running_total = lax.optimization_barrier(jnp.sum(weights, axis=1, keepdims=True))
            blended = jnp.dot(weights.astype(jnp.bfloat16), head_values, preferred_element_type=jnp.float32)
            return (blended / running_total).astype(jnp.bfloat16)
        heads_out = lax.map(one_head, jnp.arange(HEADS, dtype=jnp.int32))
        return jnp.transpose(heads_out, (1, 0, 2)).reshape(FRAME_TOK, HH)
    attention = lax.map(one_frame, jnp.arange(FRAMES, dtype=jnp.int32))
    gates = jnp.take(gate_table, timesteps, axis=0)
    updated = (residual.astype(jnp.float32) + gates[:, None, :] * attention.astype(jnp.float32)).astype(jnp.bfloat16)
    next_queue = jnp.concatenate([updated[1:], incoming[None]], axis=0)
    leaving = updated[0]
    return (next_queue, leaving)
```

```python
import functools
import math

import jax
import jax.numpy as jnp
from jax import lax
from jax.experimental import pallas as pl
from jax.experimental.pallas import tpu as pltpu
from jax.sharding import PartitionSpec as P

HD = 128
ROPE_DIMS = 16
EXP2_SCALE = math.log2(math.e) / math.sqrt(HD)
VMEM = pl.BlockSpec(memory_space=pltpu.VMEM)
SMEM = pl.BlockSpec(memory_space=pltpu.SMEM)


def shifted(block, axis, distance):
    devices = range(lax.axis_size(axis))
    route = [(i - distance, i) for i in devices if i - distance in devices]
    return lax.ppermute(block, axis, route)


def swapped(block):
    return lax.ppermute(block, "tok", [(0, 1), (1, 0)])


def pack_kernel(position_ref, q_ref, k_ref, v_ref, out_ref):
    tokens = q_ref.shape[1]
    half = ROPE_DIMS // 2
    lane = lax.broadcasted_iota(jnp.int32, (8, HD), 1)
    pair = jnp.where(lane < half, lane, lane - half)
    angle = position_ref[0].astype(jnp.float32) * jnp.exp2(-pair.astype(jnp.float32))
    turns = lane < ROPE_DIMS
    cosine = jnp.where(turns, jnp.cos(angle), 1.0)[:1]
    sine = jnp.sin(angle)
    from_second = jnp.where(lane < half, -sine, 0.0)[:1]
    from_leading = jnp.where(turns & (lane >= half), sine, 0.0)[:1]
    for head in range(out_ref.shape[0]):
        columns = slice(head * HD, (head + 1) * HD)
        for place, ref in enumerate((q_ref, k_ref)):
            x = ref[0, :, columns].astype(jnp.float32)
            turned = (
                x * cosine
                + pltpu.roll(x, HD - half, 1) * from_second
                + pltpu.roll(x, half, 1) * from_leading
            )
            out_ref[head, place * tokens : (place + 1) * tokens, :] = turned.astype(jnp.bfloat16)
        out_ref[head, 2 * tokens : 3 * tokens, :] = v_ref[0, :, columns]


def pack(positions, queries, keys, values):
    _, tokens, columns = queries.shape
    return pl.pallas_call(
        pack_kernel,
        out_shape=jax.ShapeDtypeStruct((columns // HD, 3 * tokens, HD), jnp.bfloat16),
        in_specs=[SMEM, VMEM, VMEM, VMEM],
        out_specs=VMEM,
        compiler_params=pltpu.CompilerParams(vmem_limit_bytes=16 * 2**20),
        name="pack",
    )(positions, queries, keys, values)


def attend_blocks(q_ref, pair_refs, before, after, query_rows, key_rows):
    groups, tokens, _ = q_ref.shape
    query_groups = query_rows // tokens
    key_groups = key_rows // tokens

    def one_block(index, carry):
        rows = pl.ds(pl.multiple_of(index * query_rows, query_rows), query_rows)
        q = q_ref[pl.ds(index * query_groups, query_groups)].reshape(query_rows, HD)
        chunks = [(ref, g) for ref in pair_refs for g in range(0, groups, key_groups)]

        def scores_of(chunk):
            ref, g = chunk
            k = ref[g : g + key_groups, :tokens, :].reshape(key_rows, HD)
            return lax.dot_general(
                q, k, (((1,), (1,)), ((), ())), preferred_element_type=jnp.float32
            )

        if before is None:
            highest = None
        else:
            highest, total, blended = (ref[rows, :] for ref in before)
            highest = highest[:, :1]
        scores = scores_of(chunks[0])
        for place, (ref, g) in enumerate(chunks):
            following = scores_of(chunks[place + 1]) if place + 1 < len(chunks) else None
            summit = jnp.max(scores, axis=1, keepdims=True) * EXP2_SCALE
            if highest is not None:
                summit = jnp.maximum(highest, summit)
            weights = jnp.exp2(scores * EXP2_SCALE - summit).astype(jnp.bfloat16)
            v = ref[g : g + key_groups, tokens:, :].reshape(key_rows, HD)
            both = lax.dot_general(
                weights,
                jnp.concatenate([v, jnp.ones_like(v)], axis=1),
                (((1,), (0,)), ((), ())),
                preferred_element_type=jnp.float32,
            )
            if highest is None:
                blended, total = both[:, :HD], both[:, HD:]
            else:
                factor = jnp.exp2(highest - summit)
                blended = blended * factor + both[:, :HD]
                total = total * factor + both[:, HD:]
            highest = summit
            scores = following
        for ref, result in zip(after, (jnp.broadcast_to(highest, total.shape), total, blended)):
            ref[rows, :] = result
        return carry

    lax.fori_loop(0, groups * tokens // query_rows, one_block, 0)


def own_kernel(q_ref, own_ref, peer_ref, *running, query_rows, key_rows):
    attend_blocks(q_ref, (own_ref, peer_ref), None, running, query_rows, key_rows)


def near_kernel(
    usable_ref, q_ref, highest, total, blended, *refs, query_rows, key_rows
):
    *pairs, out_ref, highest_s, total_s, blended_s = refs
    start = (highest, total, blended)
    running = (highest_s, total_s, blended_s)

    def finish(total, blended):
        out_ref[...] = (
            (blended[...] / total[...]).astype(jnp.bfloat16).reshape(out_ref.shape)
        )

    has_before, has_after = usable_ref[0] > 0, usable_ref[1] > 0

    @pl.when(has_before)
    def _():
        attend_blocks(q_ref, pairs[:2], start, running, query_rows, key_rows)

    @pl.when(jnp.logical_not(has_before))
    def _():
        for ref, given in zip(running, start):
            ref[...] = given[...]

    @pl.when(has_after)
    def _():
        attend_blocks(q_ref, pairs[2:], running, running, query_rows, key_rows)

    finish(total_s, blended_s)


def attention_of(q, own, peer, usable, near, query_rows, key_rows):
    groups, tokens, _ = q.shape
    rows = groups * tokens
    state = jax.ShapeDtypeStruct((rows, HD), jnp.float32)
    params = pltpu.CompilerParams(vmem_limit_bytes=40 * 2**20)
    sizes = dict(query_rows=query_rows, key_rows=key_rows)
    running = pl.pallas_call(
        functools.partial(own_kernel, **sizes),
        out_shape=[state] * 3,
        in_specs=[VMEM] * 3,
        out_specs=[VMEM] * 3,
        compiler_params=params,
        cost_estimate=pl.CostEstimate(
            flops=8 * rows * rows * HD, bytes_accessed=5 * rows * HD * 4, transcendentals=rows * rows
        ),
        name="attend_own",
    )(q, own, peer)
    return pl.pallas_call(
        functools.partial(near_kernel, **sizes),
        out_shape=jax.ShapeDtypeStruct(q.shape, jnp.bfloat16),
        in_specs=[SMEM] + [VMEM] * 8,
        out_specs=VMEM,
        scratch_shapes=[pltpu.VMEM((rows, HD), jnp.float32)] * 3,
        compiler_params=params,
        name="attend_near",
    )(usable, q, *running, *near)


def update_kernel(step_ref, returned_ref, residual_ref, gate_ref, updated_ref, blocks_ref):
    gate = gate_ref[pl.ds(step_ref[0], 1), :]
    for head in range(returned_ref.shape[0]):
        columns = slice(head * HD, (head + 1) * HD)
        updated = (
            residual_ref[0, :, columns].astype(jnp.float32)
            + gate[:, columns] * returned_ref[head].astype(jnp.float32)
        ).astype(jnp.bfloat16)
        updated_ref[0, :, columns] = updated
        blocks_ref[head] = updated


def update(timesteps, returned, residual, gate_table):
    return pl.pallas_call(
        update_kernel,
        out_shape=[
            jax.ShapeDtypeStruct(residual.shape, jnp.bfloat16),
            jax.ShapeDtypeStruct(returned.shape, jnp.bfloat16),
        ],
        in_specs=[SMEM, VMEM, VMEM, VMEM],
        out_specs=[VMEM, VMEM],
        compiler_params=pltpu.CompilerParams(vmem_limit_bytes=16 * 2**20),
        name="update",
    )(timesteps, returned, residual, gate_table)


def per_device(queries, keys, values, residual, incoming, gate_table, timesteps, positions):
    tokens = queries.shape[1]
    frame_index = lax.axis_index("frame")
    last_index = lax.axis_size("frame") - 1
    packed = pack(positions, queries, keys, values)
    received = lax.all_to_all(packed, "head", split_axis=0, concat_axis=0, tiled=True)
    q, own = received[:, :tokens], received[:, tokens:]
    prior = shifted(own, "frame", 1)
    later = shifted(own, "frame", -1)
    peer = swapped(own)
    near = (prior, swapped(prior), later, swapped(later))
    usable = jnp.stack([frame_index > 0, frame_index < last_index]).astype(jnp.int32)
    attention = attention_of(q, own, peer, usable, near, 384, 1536)
    returned = lax.all_to_all(attention, "head", split_axis=0, concat_axis=0, tiled=True)
    updated, blocks = update(timesteps, returned, residual, gate_table)
    arriving = shifted(updated, "frame", -1)
    departed = lax.all_to_all(blocks, "frame", split_axis=0, concat_axis=0, tiled=True)
    next_queue = jnp.where(frame_index == last_index, incoming[None], arriving)
    return (next_queue, departed[0])


def solution(mesh):
    placed = (
        P("frame", ("head", "tok"), None),
        P("frame", ("head", "tok"), None),
        P("frame", ("head", "tok"), None),
        P("frame", ("head", "tok"), None),
        P(("head", "tok"), None),
        P(),
        P("frame"),
        P("frame"),
    )
    return jax.shard_map(
        per_device,
        mesh=mesh,
        in_specs=placed,
        out_specs=(P("frame", ("head", "tok"), None), P(("head", "tok"), "frame")),
        check_vma=False,
    )
```

```python
import functools
import math

import jax
import jax.numpy as jnp
from jax import lax
from jax.experimental import pallas as pl
from jax.experimental.pallas import tpu as pltpu
from jax.sharding import PartitionSpec as P

HD = 128
ROPE_DIMS = 16
EXP2_SCALE = math.log2(math.e) / math.sqrt(HD)
VMEM = pl.BlockSpec(memory_space=pltpu.VMEM)
SMEM = pl.BlockSpec(memory_space=pltpu.SMEM)


def shifted(block, axis, distance):
    devices = range(lax.axis_size(axis))
    route = [(i - distance, i) for i in devices if i - distance in devices]
    return lax.ppermute(block, axis, route)


def swapped(block):
    return lax.ppermute(block, "tok", [(0, 1), (1, 0)])


def rotation(position):
    half = ROPE_DIMS // 2
    lane = lax.broadcasted_iota(jnp.int32, (8, HD), 1)
    pair = jnp.where(lane < half, lane, lane - half)
    angle = position.astype(jnp.float32) * jnp.exp2(-pair.astype(jnp.float32))
    turns = lane < ROPE_DIMS
    sine = jnp.sin(angle)
    own = jnp.where(turns, jnp.cos(angle), 1.0)[:1]
    ahead = jnp.where(lane < half, -sine, 0.0)[:1]
    behind = jnp.where(turns & (lane >= half), sine, 0.0)[:1]
    return own, ahead, behind


def rotate(x, factors):
    own, ahead, behind = factors
    half = ROPE_DIMS // 2
    x = x.astype(jnp.float32)
    turned = x * own + pltpu.roll(x, HD - half, 1) * ahead + pltpu.roll(x, half, 1) * behind
    return turned.astype(jnp.bfloat16)


def pack_kernel(position_ref, turned_ref, *refs):
    *kept_refs, out_ref = refs
    tokens = turned_ref.shape[1]
    factors = rotation(position_ref[0])
    for head in range(out_ref.shape[0]):
        columns = slice(head * HD, (head + 1) * HD)
        out_ref[head, :tokens, :] = rotate(turned_ref[0, :, columns], factors)
        for kept_ref in kept_refs:
            out_ref[head, tokens:, :] = kept_ref[0, :, columns]


def pack(positions, *arrays):
    _, tokens, columns = arrays[0].shape
    heads = 8
    block = pl.BlockSpec((1, tokens, heads * HD), lambda i: (0, 0, i))
    rows = len(arrays) * tokens
    return pl.pallas_call(
        pack_kernel,
        grid=(columns // HD // heads,),
        out_shape=jax.ShapeDtypeStruct((columns // HD, rows, HD), jnp.bfloat16),
        in_specs=[SMEM] + [block] * len(arrays),
        out_specs=pl.BlockSpec((heads, rows, HD), lambda i: (i, 0, 0)),
        compiler_params=pltpu.CompilerParams(vmem_limit_bytes=60 * 2**20),
        name="pack",
    )(positions, *arrays)


def attend_block(q, pair_refs, key_rows, refs_at_once):
    def scores_of(refs):
        return [
            lax.dot_general(
                q,
                ref[:, : ref.shape[1] // 2, :].reshape(key_rows, HD),
                (((1,), (1,)), ((), ())),
                preferred_element_type=jnp.float32,
            )
            for ref in refs
        ]

    steps = [
        pair_refs[place : place + refs_at_once]
        for place in range(0, len(pair_refs), refs_at_once)
    ]
    scores = scores_of(steps[0])
    for place, refs in enumerate(steps):
        following = scores_of(steps[place + 1]) if place + 1 < len(steps) else None
        summit = functools.reduce(jnp.maximum, scores)
        summit = jnp.max(summit, axis=1, keepdims=True) * EXP2_SCALE
        if place:
            summit = jnp.maximum(highest, summit)
        both = None
        for part, ref in zip(scores, refs):
            weights = jnp.exp2(part * EXP2_SCALE - summit).astype(jnp.bfloat16)
            v = ref[:, ref.shape[1] // 2 :, :].reshape(key_rows, HD)
            product = lax.dot_general(
                weights,
                jnp.concatenate([v, jnp.ones_like(v)], axis=1),
                (((1,), (0,)), ((), ())),
                preferred_element_type=jnp.float32,
            )
            both = product if both is None else both + product
        running = running * jnp.exp2(highest - summit) + both if place else both
        highest = summit
        scores = following
    return (running[:, :HD] / running[:, HD:]).astype(jnp.bfloat16)


def attend_kernel(usable_ref, q_ref, *refs, query_rows):
    *pairs, out_ref = refs
    groups, tokens, _ = q_ref.shape
    query_groups = query_rows // tokens

    def all_blocks(pair_refs):
        def one_block(index, carry):
            block = pl.ds(index * query_groups, query_groups)
            q = q_ref[block].reshape(query_rows, HD)
            found = attend_block(q, pair_refs, groups * tokens, 2)
            out_ref[block] = found.reshape(query_groups, tokens, HD)
            return carry

        lax.fori_loop(0, groups // query_groups, one_block, 0)

    has_before, has_after = usable_ref[0] > 0, usable_ref[1] > 0

    @pl.when(has_before & has_after)
    def _():
        all_blocks(pairs)

    @pl.when(jnp.logical_not(has_before))
    def _():
        all_blocks(pairs[:2] + pairs[4:])

    @pl.when(jnp.logical_not(has_after))
    def _():
        all_blocks(pairs[:4])


def attend(usable, q, pairs, **sizes):
    groups, tokens, _ = q.shape
    rows = groups * tokens
    return pl.pallas_call(
        functools.partial(attend_kernel, **sizes),
        out_shape=jax.ShapeDtypeStruct(q.shape, jnp.bfloat16),
        in_specs=[SMEM] + [VMEM] * (1 + len(pairs)),
        out_specs=VMEM,
        compiler_params=pltpu.CompilerParams(vmem_limit_bytes=40 * 2**20),
        cost_estimate=pl.CostEstimate(
            flops=24 * rows * rows * HD,
            bytes_accessed=28 * rows * HD,
            transcendentals=6 * rows * rows,
        ),
        name="attend",
    )(usable, q, *pairs)


def update_kernel(
    step_ref, first_ref, returned_ref, residual_ref, incoming_ref, gate_ref, moving_ref, *parts
):
    gate = gate_ref[pl.ds(step_ref[0], 1), :]
    heads = parts[0].shape[0]
    first = first_ref[0] > 0
    for head in range(returned_ref.shape[0]):
        columns = slice(head * HD, (head + 1) * HD)
        updated = (
            residual_ref[0, :, columns].astype(jnp.float32)
            + gate[:, columns] * returned_ref[head].astype(jnp.float32)
        ).astype(jnp.bfloat16)
        moving_ref[0, :, columns] = jnp.where(first, incoming_ref[:, columns], updated)
        parts[head // heads][head % heads] = updated


def update(timesteps, first, returned, residual, incoming, gate_table):
    heads, tokens, _ = returned.shape
    part = jax.ShapeDtypeStruct((heads // 4, tokens, HD), jnp.bfloat16)
    moving, *parts = pl.pallas_call(
        update_kernel,
        out_shape=[jax.ShapeDtypeStruct(residual.shape, jnp.bfloat16)] + [part] * 4,
        in_specs=[SMEM, SMEM, VMEM, VMEM, VMEM, VMEM],
        out_specs=[VMEM] * 5,
        compiler_params=pltpu.CompilerParams(vmem_limit_bytes=16 * 2**20),
        name="update",
    )(timesteps, first, returned, residual, incoming, gate_table)
    return moving, parts


def spread(parts, axis):
    size = lax.axis_size(axis)
    step = len(parts)
    index = lax.axis_index(axis)
    firsts = [lax.ppermute(parts[a], axis, [(0, a * step)]) for a in range(1, step)]
    held = jnp.where(index == 0, parts[0], sum(firsts))
    seconds = [
        lax.ppermute(held[b], axis, [(a, a + b) for a in range(0, size, step)])
        for b in range(1, step)
    ]
    return jnp.where(index % step == 0, held[0], sum(seconds))


def per_device(queries, keys, values, residual, incoming, gate_table, timesteps, positions):
    frame_index = lax.axis_index("frame")
    frames = lax.axis_size("frame")
    own = lax.all_to_all(
        pack(positions, keys, values), "head", split_axis=0, concat_axis=0, tiled=True
    )
    own, packed = lax.optimization_barrier((own, pack(positions, queries)))
    prior = shifted(own, "frame", 1)
    later = shifted(own, "frame", -1)
    q = lax.all_to_all(packed, "head", split_axis=0, concat_axis=0, tiled=True)
    pairs = (own, swapped(own), prior, swapped(prior), later, swapped(later))
    usable = jnp.stack([frame_index > 0, frame_index < frames - 1]).astype(jnp.int32)
    attention = attend(usable, q, pairs, query_rows=384)
    returned = lax.all_to_all(attention, "head", split_axis=0, concat_axis=0, tiled=True)
    first = (frame_index == 0).astype(jnp.int32)[None]
    moving, parts = update(timesteps, first, returned, residual, incoming, gate_table)
    next_queue = lax.ppermute(moving, "frame", [(i, (i - 1) % frames) for i in range(frames)])
    return (next_queue, spread(parts, "frame"))


def solution(mesh):
    placed = (
        P("frame", ("head", "tok"), None),
        P("frame", ("head", "tok"), None),
        P("frame", ("head", "tok"), None),
        P("frame", ("head", "tok"), None),
        P(("head", "tok"), None),
        P(),
        P("frame"),
        P("frame"),
    )
    return jax.shard_map(
        per_device,
        mesh=mesh,
        in_specs=placed,
        out_specs=(P("frame", ("head", "tok"), None), P(("head", "tok"), "frame")),
        check_vma=False,
    )
```

```python
import functools
import math

import jax
import jax.numpy as jnp
from jax import lax
from jax.experimental import pallas as pl
from jax.experimental.pallas import tpu as pltpu
from jax.sharding import PartitionSpec as P

HD = 128
ROPE_DIMS = 16
EXP2_SCALE = math.log2(math.e) / math.sqrt(HD)
VMEM = pl.BlockSpec(memory_space=pltpu.VMEM)
SMEM = pl.BlockSpec(memory_space=pltpu.SMEM)


def shifted(block, axis, distance):
    devices = range(lax.axis_size(axis))
    route = [(i - distance, i) for i in devices if i - distance in devices]
    return lax.ppermute(block, axis, route)


def swapped(block):
    return lax.ppermute(block, "tok", [(0, 1), (1, 0)])


def rotation(position):
    half = ROPE_DIMS // 2
    lane = lax.broadcasted_iota(jnp.int32, (8, HD), 1)
    pair = jnp.where(lane < half, lane, lane - half)
    angle = position.astype(jnp.float32) * jnp.exp2(-pair.astype(jnp.float32))
    turns = lane < ROPE_DIMS
    sine = jnp.sin(angle)
    own = jnp.where(turns, jnp.cos(angle), 1.0)[:1]
    ahead = jnp.where(lane < half, -sine, 0.0)[:1]
    behind = jnp.where(turns & (lane >= half), sine, 0.0)[:1]
    return own, ahead, behind


def rotate(x, factors):
    own, ahead, behind = factors
    half = ROPE_DIMS // 2
    x = x.astype(jnp.float32)
    turned = x * own + pltpu.roll(x, HD - half, 1) * ahead + pltpu.roll(x, half, 1) * behind
    return turned.astype(jnp.bfloat16)


def pack_kernel(position_ref, turned_ref, *refs):
    *kept_refs, out_ref = refs
    tokens = turned_ref.shape[1]
    factors = rotation(position_ref[0])
    for head in range(out_ref.shape[0]):
        columns = slice(head * HD, (head + 1) * HD)
        out_ref[head, :tokens, :] = rotate(turned_ref[0, :, columns], factors)
        for kept_ref in kept_refs:
            out_ref[head, tokens:, :] = kept_ref[0, :, columns]


def pack(positions, *arrays):
    _, tokens, columns = arrays[0].shape
    heads = 8
    block = pl.BlockSpec((1, tokens, heads * HD), lambda i: (0, 0, i))
    rows = len(arrays) * tokens
    return pl.pallas_call(
        pack_kernel,
        grid=(columns // HD // heads,),
        out_shape=jax.ShapeDtypeStruct((columns // HD, rows, HD), jnp.bfloat16),
        in_specs=[SMEM] + [block] * len(arrays),
        out_specs=pl.BlockSpec((heads, rows, HD), lambda i: (i, 0, 0)),
        compiler_params=pltpu.CompilerParams(vmem_limit_bytes=60 * 2**20),
        name="pack",
    )(positions, *arrays)


def attend_block(q, pair_refs, key_rows, refs_at_once):
    def scores_of(refs):
        return [
            lax.dot_general(
                q,
                ref[:, : ref.shape[1] // 2, :].reshape(key_rows, HD),
                (((1,), (1,)), ((), ())),
                preferred_element_type=jnp.float32,
            )
            for ref in refs
        ]

    steps = [
        pair_refs[place : place + refs_at_once]
        for place in range(0, len(pair_refs), refs_at_once)
    ]
    scores = scores_of(steps[0])
    for place, refs in enumerate(steps):
        following = scores_of(steps[place + 1]) if place + 1 < len(steps) else None
        summit = functools.reduce(jnp.maximum, scores)
        summit = jnp.max(summit, axis=1, keepdims=True) * EXP2_SCALE
        if place:
            summit = jnp.maximum(highest, summit)
        both = None
        for part, ref in zip(scores, refs):
            weights = jnp.exp2(part * EXP2_SCALE - summit).astype(jnp.bfloat16)
            v = ref[:, ref.shape[1] // 2 :, :].reshape(key_rows, HD)
            product = lax.dot_general(
                weights,
                jnp.concatenate([v, jnp.ones_like(v)], axis=1),
                (((1,), (0,)), ((), ())),
                preferred_element_type=jnp.float32,
            )
            both = product if both is None else both + product
        running = running * jnp.exp2(highest - summit) + both if place else both
        highest = summit
        scores = following
    return (running[:, :HD] / running[:, HD:]).astype(jnp.bfloat16)


def attend_kernel(usable_ref, q_ref, *refs, query_rows):
    *pairs, out_ref = refs
    groups, tokens, _ = q_ref.shape
    query_groups = query_rows // tokens

    def all_blocks(pair_refs):
        def one_block(index, carry):
            block = pl.ds(index * query_groups, query_groups)
            q = q_ref[block].reshape(query_rows, HD)
            found = attend_block(q, pair_refs, groups * tokens, 2)
            out_ref[block] = found.reshape(query_groups, tokens, HD)
            return carry

        lax.fori_loop(0, groups // query_groups, one_block, 0)

    has_before, has_after = usable_ref[0] > 0, usable_ref[1] > 0

    @pl.when(has_before & has_after)
    def _():
        all_blocks(pairs)

    @pl.when(jnp.logical_not(has_before))
    def _():
        all_blocks(pairs[:2] + pairs[4:])

    @pl.when(jnp.logical_not(has_after))
    def _():
        all_blocks(pairs[:4])


def attend(usable, q, pairs, **sizes):
    groups, tokens, _ = q.shape
    rows = groups * tokens
    return pl.pallas_call(
        functools.partial(attend_kernel, **sizes),
        out_shape=jax.ShapeDtypeStruct(q.shape, jnp.bfloat16),
        in_specs=[SMEM] + [VMEM] * (1 + len(pairs)),
        out_specs=VMEM,
        compiler_params=pltpu.CompilerParams(vmem_limit_bytes=26 * 2**20),
        cost_estimate=pl.CostEstimate(
            flops=24 * rows * rows * HD,
            bytes_accessed=28 * rows * HD,
            transcendentals=6 * rows * rows,
        ),
        name="attend",
    )(usable, q, *pairs)


def update_kernel(
    step_ref, first_ref, returned_ref, residual_ref, incoming_ref, gate_ref, moving_ref, *parts
):
    gate = gate_ref[pl.ds(step_ref[0], 1), :]
    heads = parts[0].shape[0]
    first = first_ref[0] > 0
    for head in range(returned_ref.shape[0]):
        columns = slice(head * HD, (head + 1) * HD)
        updated = (
            residual_ref[0, :, columns].astype(jnp.float32)
            + gate[:, columns] * returned_ref[head].astype(jnp.float32)
        ).astype(jnp.bfloat16)
        moving_ref[0, :, columns] = jnp.where(first, incoming_ref[:, columns], updated)
        parts[head // heads][head % heads] = updated


def update(timesteps, first, returned, residual, incoming, gate_table):
    heads, tokens, _ = returned.shape
    part = jax.ShapeDtypeStruct((heads // 4, tokens, HD), jnp.bfloat16)
    moving, *parts = pl.pallas_call(
        update_kernel,
        out_shape=[jax.ShapeDtypeStruct(residual.shape, jnp.bfloat16)] + [part] * 4,
        in_specs=[SMEM, SMEM, VMEM, VMEM, VMEM, VMEM],
        out_specs=[VMEM] * 5,
        compiler_params=pltpu.CompilerParams(vmem_limit_bytes=16 * 2**20),
        name="update",
    )(timesteps, first, returned, residual, incoming, gate_table)
    return moving, parts


def finish_kernel(leads_ref, moved_ref, own_ref, *refs):
    *others, next_ref, leaving_ref = refs
    next_ref[...] = moved_ref[...]
    passed = sum(ref[...].astype(jnp.float32) for ref in others).astype(jnp.bfloat16)
    leaving_ref[...] = jnp.where(leads_ref[0] > 0, own_ref[...], passed)


def finish(leads, moved, own, others):
    return pl.pallas_call(
        finish_kernel,
        out_shape=[
            jax.ShapeDtypeStruct(moved.shape, moved.dtype),
            jax.ShapeDtypeStruct(own.shape, own.dtype),
        ],
        in_specs=[SMEM] + [VMEM] * (2 + len(others)),
        out_specs=[VMEM, VMEM],
        compiler_params=pltpu.CompilerParams(vmem_limit_bytes=16 * 2**20),
        name="finish",
    )(leads, moved, own, *others)


def spread(parts, axis):
    size = lax.axis_size(axis)
    step = len(parts)
    index = lax.axis_index(axis)
    firsts = [lax.ppermute(parts[a], axis, [(0, a * step)]) for a in range(1, step)]
    held = jnp.where(index == 0, parts[0], sum(firsts))
    seconds = [
        lax.ppermute(held[b], axis, [(a, a + b) for a in range(0, size, step)])
        for b in range(1, step)
    ]
    return held[0], seconds


def per_device(queries, keys, values, residual, incoming, gate_table, timesteps, positions):
    frame_index = lax.axis_index("frame")
    frames = lax.axis_size("frame")
    own = lax.all_to_all(
        pack(positions, keys, values), "head", split_axis=0, concat_axis=0, tiled=True
    )
    own, packed = lax.optimization_barrier((own, pack(positions, queries)))
    prior = shifted(own, "frame", 1)
    later = shifted(own, "frame", -1)
    q = lax.all_to_all(packed, "head", split_axis=0, concat_axis=0, tiled=True)
    pairs = (own, swapped(own), prior, swapped(prior), later, swapped(later))
    usable = jnp.stack([frame_index > 0, frame_index < frames - 1]).astype(jnp.int32)
    attention = attend(usable, q, pairs, query_rows=384)
    returned = lax.all_to_all(attention, "head", split_axis=0, concat_axis=0, tiled=True)
    first = (frame_index == 0).astype(jnp.int32)[None]
    moving, parts = update(timesteps, first, returned, residual, incoming, gate_table)
    next_queue = lax.ppermute(moving, "frame", [(i, (i - 1) % frames) for i in range(frames)])
    held, sent = spread(parts, "frame")
    leads = (frame_index % len(parts) == 0).astype(jnp.int32)[None]
    return tuple(finish(leads, next_queue, held, sent))


def solution(mesh):
    placed = (
        P("frame", ("head", "tok"), None),
        P("frame", ("head", "tok"), None),
        P("frame", ("head", "tok"), None),
        P("frame", ("head", "tok"), None),
        P(("head", "tok"), None),
        P(),
        P("frame"),
        P("frame"),
    )
    return jax.shard_map(
        per_device,
        mesh=mesh,
        in_specs=placed,
        out_specs=(P("frame", ("head", "tok"), None), P(("head", "tok"), "frame")),
        check_vma=False,
    )
```

```python
import functools
import math

import jax
import jax.numpy as jnp
from jax import lax
from jax.experimental import pallas as pl
from jax.experimental.pallas import tpu as pltpu
from jax.sharding import PartitionSpec as P

HD = 128
ROPE_DIMS = 16
EXP2_SCALE = math.log2(math.e) / math.sqrt(HD)
VMEM = pl.BlockSpec(memory_space=pltpu.VMEM)
SMEM = pl.BlockSpec(memory_space=pltpu.SMEM)


def shifted(block, axis, distance):
    devices = range(lax.axis_size(axis))
    route = [(i - distance, i) for i in devices if i - distance in devices]
    return lax.ppermute(block, axis, route)


def swapped(block):
    return lax.ppermute(block, "tok", [(0, 1), (1, 0)])


def rotation(position):
    half = ROPE_DIMS // 2
    lane = lax.broadcasted_iota(jnp.int32, (8, HD), 1)
    pair = jnp.where(lane < half, lane, lane - half)
    angle = position.astype(jnp.float32) * jnp.exp2(-pair.astype(jnp.float32))
    turns = lane < ROPE_DIMS
    sine = jnp.sin(angle)
    own = jnp.where(turns, jnp.cos(angle), 1.0)[:1]
    ahead = jnp.where(lane < half, -sine, 0.0)[:1]
    behind = jnp.where(turns & (lane >= half), sine, 0.0)[:1]
    return own, ahead, behind


def rotate(x, factors):
    own, ahead, behind = factors
    half = ROPE_DIMS // 2
    x = x.astype(jnp.float32)
    turned = x * own + pltpu.roll(x, HD - half, 1) * ahead + pltpu.roll(x, half, 1) * behind
    return turned.astype(jnp.bfloat16)


def pack_kernel(position_ref, turned_ref, *refs):
    *kept_refs, out_ref = refs
    tokens = turned_ref.shape[1]
    factors = rotation(position_ref[0])
    for head in range(out_ref.shape[0]):
        columns = slice(head * HD, (head + 1) * HD)
        out_ref[head, :tokens, :] = rotate(turned_ref[0, :, columns], factors)
        for kept_ref in kept_refs:
            out_ref[head, tokens:, :] = kept_ref[0, :, columns]


def pack(positions, *arrays):
    _, tokens, columns = arrays[0].shape
    heads = 8
    block = pl.BlockSpec((1, tokens, heads * HD), lambda i: (0, 0, i))
    rows = len(arrays) * tokens
    return pl.pallas_call(
        pack_kernel,
        grid=(columns // HD // heads,),
        out_shape=jax.ShapeDtypeStruct((columns // HD, rows, HD), jnp.bfloat16),
        in_specs=[SMEM] + [block] * len(arrays),
        out_specs=pl.BlockSpec((heads, rows, HD), lambda i: (i, 0, 0)),
        compiler_params=pltpu.CompilerParams(vmem_limit_bytes=60 * 2**20),
        name="pack",
    )(positions, *arrays)


def attend_block(q, pair_refs, key_rows, refs_at_once):
    def scores_of(refs):
        return [
            lax.dot_general(
                q,
                ref[:, : ref.shape[1] // 2, :].reshape(key_rows, HD),
                (((1,), (1,)), ((), ())),
                preferred_element_type=jnp.float32,
            )
            for ref in refs
        ]

    steps = [
        pair_refs[place : place + refs_at_once]
        for place in range(0, len(pair_refs), refs_at_once)
    ]
    scores = scores_of(steps[0])
    for place, refs in enumerate(steps):
        following = scores_of(steps[place + 1]) if place + 1 < len(steps) else None
        summit = functools.reduce(jnp.maximum, scores)
        summit = jnp.max(summit, axis=1, keepdims=True) * EXP2_SCALE
        if place:
            summit = jnp.maximum(highest, summit)
        both = None
        for part, ref in zip(scores, refs):
            weights = jnp.exp2(part * EXP2_SCALE - summit).astype(jnp.bfloat16)
            v = ref[:, ref.shape[1] // 2 :, :].reshape(key_rows, HD)
            product = lax.dot_general(
                weights,
                jnp.concatenate([v, jnp.ones_like(v)], axis=1),
                (((1,), (0,)), ((), ())),
                preferred_element_type=jnp.float32,
            )
            both = product if both is None else both + product
        running = running * jnp.exp2(highest - summit) + both if place else both
        highest = summit
        scores = following
    return (running[:, :HD] / running[:, HD:]).astype(jnp.bfloat16)


def attend_kernel(usable_ref, q_ref, *refs, query_rows):
    *pairs, out_ref = refs
    groups, tokens, _ = q_ref.shape
    query_groups = query_rows // tokens

    def all_blocks(pair_refs):
        def one_block(index, carry):
            block = pl.ds(index * query_groups, query_groups)
            q = q_ref[block].reshape(query_rows, HD)
            found = attend_block(q, pair_refs, groups * tokens, 2)
            out_ref[block] = found.reshape(query_groups, tokens, HD)
            return carry

        lax.fori_loop(0, groups // query_groups, one_block, 0)

    has_before, has_after = usable_ref[0] > 0, usable_ref[1] > 0

    @pl.when(has_before & has_after)
    def _():
        all_blocks(pairs)

    @pl.when(jnp.logical_not(has_before))
    def _():
        all_blocks(pairs[:2] + pairs[4:])

    @pl.when(jnp.logical_not(has_after))
    def _():
        all_blocks(pairs[:4])


def attend(usable, q, pairs, **sizes):
    groups, tokens, _ = q.shape
    rows = groups * tokens
    return pl.pallas_call(
        functools.partial(attend_kernel, **sizes),
        out_shape=jax.ShapeDtypeStruct(q.shape, jnp.bfloat16),
        in_specs=[SMEM] + [VMEM] * (1 + len(pairs)),
        out_specs=VMEM,
        compiler_params=pltpu.CompilerParams(vmem_limit_bytes=60 * 2**20),
        cost_estimate=pl.CostEstimate(
            flops=24 * rows * rows * HD,
            bytes_accessed=28 * rows * HD,
            transcendentals=6 * rows * rows,
        ),
        name="attend",
    )(usable, q, *pairs)


def update_kernel(
    step_ref, first_ref, returned_ref, residual_ref, incoming_ref, gate_ref, moving_ref, *parts
):
    gate = gate_ref[pl.ds(step_ref[0], 1), :]
    heads = parts[0].shape[0]
    first = first_ref[0] > 0
    for head in range(returned_ref.shape[0]):
        columns = slice(head * HD, (head + 1) * HD)
        updated = (
            residual_ref[0, :, columns].astype(jnp.float32)
            + gate[:, columns] * returned_ref[head].astype(jnp.float32)
        ).astype(jnp.bfloat16)
        moving_ref[0, :, columns] = jnp.where(first, incoming_ref[:, columns], updated)
        parts[head // heads][head % heads] = updated


def update(timesteps, first, returned, residual, incoming, gate_table):
    heads, tokens, _ = returned.shape
    part = jax.ShapeDtypeStruct((heads // 4, tokens, HD), jnp.bfloat16)
    moving, *parts = pl.pallas_call(
        update_kernel,
        out_shape=[jax.ShapeDtypeStruct(residual.shape, jnp.bfloat16)] + [part] * 4,
        in_specs=[SMEM, SMEM, VMEM, VMEM, VMEM, VMEM],
        out_specs=[VMEM] * 5,
        compiler_params=pltpu.CompilerParams(vmem_limit_bytes=16 * 2**20),
        name="update",
    )(timesteps, first, returned, residual, incoming, gate_table)
    return moving, parts


def finish_kernel(leads_ref, moved_ref, own_ref, *refs):
    *others, next_ref, leaving_ref = refs
    next_ref[...] = moved_ref[...]
    passed = sum(ref[...].astype(jnp.float32) for ref in others).astype(jnp.bfloat16)
    leaving_ref[...] = jnp.where(leads_ref[0] > 0, own_ref[...], passed)


def finish(leads, moved, own, others):
    return pl.pallas_call(
        finish_kernel,
        out_shape=[
            jax.ShapeDtypeStruct(moved.shape, moved.dtype),
            jax.ShapeDtypeStruct(own.shape, own.dtype),
        ],
        in_specs=[SMEM] + [VMEM] * (2 + len(others)),
        out_specs=[VMEM, VMEM],
        compiler_params=pltpu.CompilerParams(vmem_limit_bytes=16 * 2**20),
        name="finish",
    )(leads, moved, own, *others)


def spread(parts, axis):
    size = lax.axis_size(axis)
    step = len(parts)
    index = lax.axis_index(axis)
    firsts = [lax.ppermute(parts[a], axis, [(0, a * step)]) for a in range(1, step)]
    held = jnp.where(index == 0, parts[0], sum(firsts))
    seconds = [
        lax.ppermute(held[b], axis, [(a, a + b) for a in range(0, size, step)])
        for b in range(1, step)
    ]
    return held[0], seconds


def per_device(queries, keys, values, residual, incoming, gate_table, timesteps, positions):
    frame_index = lax.axis_index("frame")
    frames = lax.axis_size("frame")
    own = lax.all_to_all(
        pack(positions, keys, values), "head", split_axis=0, concat_axis=0, tiled=True
    )
    own, packed = lax.optimization_barrier((own, pack(positions, queries)))
    prior = shifted(own, "frame", 1)
    later = shifted(own, "frame", -1)
    q = lax.all_to_all(packed, "head", split_axis=0, concat_axis=0, tiled=True)
    pairs = (own, swapped(own), prior, swapped(prior), later, swapped(later))
    usable = jnp.stack([frame_index > 0, frame_index < frames - 1]).astype(jnp.int32)
    attention = attend(usable, q, pairs, query_rows=768)
    returned = lax.all_to_all(attention, "head", split_axis=0, concat_axis=0, tiled=True)
    first = (frame_index == 0).astype(jnp.int32)[None]
    moving, parts = update(timesteps, first, returned, residual, incoming, gate_table)
    next_queue = lax.ppermute(moving, "frame", [(i, (i - 1) % frames) for i in range(frames)])
    held, sent = spread(parts, "frame")
    leads = (frame_index % len(parts) == 0).astype(jnp.int32)[None]
    return tuple(finish(leads, next_queue, held, sent))


def solution(mesh):
    placed = (
        P("frame", ("head", "tok"), None),
        P("frame", ("head", "tok"), None),
        P("frame", ("head", "tok"), None),
        P("frame", ("head", "tok"), None),
        P(("head", "tok"), None),
        P(),
        P("frame"),
        P("frame"),
    )
    return jax.shard_map(
        per_device,
        mesh=mesh,
        in_specs=placed,
        out_specs=(P("frame", ("head", "tok"), None), P(("head", "tok"), "frame")),
        check_vma=False,
    )
```

```python
import functools
import math

import jax
import jax.numpy as jnp
from jax import lax
from jax.experimental import pallas as pl
from jax.experimental.pallas import tpu as pltpu
from jax.sharding import PartitionSpec as P

HD = 128
ROPE_DIMS = 16
EXP2_SCALE = math.log2(math.e) / math.sqrt(HD)
VMEM = pl.BlockSpec(memory_space=pltpu.VMEM)
SMEM = pl.BlockSpec(memory_space=pltpu.SMEM)


def shifted(block, axis, distance):
    devices = range(lax.axis_size(axis))
    route = [(i - distance, i) for i in devices if i - distance in devices]
    return lax.ppermute(block, axis, route)


def swapped(block):
    return lax.ppermute(block, "tok", [(0, 1), (1, 0)])


def rotation(position):
    half = ROPE_DIMS // 2
    lane = lax.broadcasted_iota(jnp.int32, (8, HD), 1)
    pair = jnp.where(lane < half, lane, lane - half)
    angle = position.astype(jnp.float32) * jnp.exp2(-pair.astype(jnp.float32))
    turns = lane < ROPE_DIMS
    sine = jnp.sin(angle)
    own = jnp.where(turns, jnp.cos(angle), 1.0)[:1]
    ahead = jnp.where(lane < half, -sine, 0.0)[:1]
    behind = jnp.where(turns & (lane >= half), sine, 0.0)[:1]
    return own, ahead, behind


def rotate(x, factors):
    own, ahead, behind = factors
    half = ROPE_DIMS // 2
    x = x.astype(jnp.float32)
    turned = x * own + pltpu.roll(x, HD - half, 1) * ahead + pltpu.roll(x, half, 1) * behind
    return turned.astype(jnp.bfloat16)


def pack_kernel(position_ref, turned_ref, *refs):
    *kept_refs, out_ref = refs
    tokens = turned_ref.shape[1]
    factors = rotation(position_ref[0])
    for head in range(out_ref.shape[0]):
        columns = slice(head * HD, (head + 1) * HD)
        out_ref[head, :tokens, :] = rotate(turned_ref[0, :, columns], factors)
        for kept_ref in kept_refs:
            out_ref[head, tokens:, :] = kept_ref[0, :, columns]


def pack(positions, *arrays):
    _, tokens, columns = arrays[0].shape
    heads = 8
    block = pl.BlockSpec((1, tokens, heads * HD), lambda i: (0, 0, i))
    rows = len(arrays) * tokens
    return pl.pallas_call(
        pack_kernel,
        grid=(columns // HD // heads,),
        out_shape=jax.ShapeDtypeStruct((columns // HD, rows, HD), jnp.bfloat16),
        in_specs=[SMEM] + [block] * len(arrays),
        out_specs=pl.BlockSpec((heads, rows, HD), lambda i: (i, 0, 0)),
        compiler_params=pltpu.CompilerParams(vmem_limit_bytes=60 * 2**20),
        name="pack",
    )(positions, *arrays)


def attend_block(q, pair_refs, key_rows, refs_at_once):
    def scores_of(refs):
        return [
            lax.dot_general(
                q,
                ref[:, : ref.shape[1] // 2, :].reshape(key_rows, HD),
                (((1,), (1,)), ((), ())),
                preferred_element_type=jnp.float32,
            )
            for ref in refs
        ]

    steps = [
        pair_refs[place : place + refs_at_once]
        for place in range(0, len(pair_refs), refs_at_once)
    ]
    scores = scores_of(steps[0])
    for place, refs in enumerate(steps):
        following = scores_of(steps[place + 1]) if place + 1 < len(steps) else None
        summit = functools.reduce(jnp.maximum, scores)
        summit = jnp.max(summit, axis=1, keepdims=True) * EXP2_SCALE
        if place:
            summit = jnp.maximum(highest, summit)
        both = None
        for part, ref in zip(scores, refs):
            weights = jnp.exp2(part * EXP2_SCALE - summit).astype(jnp.bfloat16)
            v = ref[:, ref.shape[1] // 2 :, :].reshape(key_rows, HD)
            product = lax.dot_general(
                weights,
                jnp.concatenate([v, jnp.ones_like(v)], axis=1),
                (((1,), (0,)), ((), ())),
                preferred_element_type=jnp.float32,
            )
            both = product if both is None else both + product
        running = running * jnp.exp2(highest - summit) + both if place else both
        highest = summit
        scores = following
    return (running[:, :HD] / running[:, HD:]).astype(jnp.bfloat16)


def attend_kernel(usable_ref, q_ref, *refs, query_rows):
    *pairs, out_ref = refs
    groups, tokens, _ = q_ref.shape
    query_groups = query_rows // tokens

    def all_blocks(pair_refs):
        def one_block(index, carry):
            block = pl.ds(index * query_groups, query_groups)
            q = q_ref[block].reshape(query_rows, HD)
            found = attend_block(q, pair_refs, groups * tokens, 2)
            out_ref[block] = found.reshape(query_groups, tokens, HD)
            return carry

        lax.fori_loop(0, groups // query_groups, one_block, 0)

    has_before, has_after = usable_ref[0] > 0, usable_ref[1] > 0

    @pl.when(has_before & has_after)
    def _():
        all_blocks(pairs)

    @pl.when(jnp.logical_not(has_before))
    def _():
        all_blocks(pairs[:2] + pairs[4:])

    @pl.when(jnp.logical_not(has_after))
    def _():
        all_blocks(pairs[:4])


def attend(usable, q, pairs, **sizes):
    groups, tokens, _ = q.shape
    rows = groups * tokens
    return pl.pallas_call(
        functools.partial(attend_kernel, **sizes),
        out_shape=jax.ShapeDtypeStruct(q.shape, jnp.bfloat16),
        in_specs=[SMEM] + [VMEM] * (1 + len(pairs)),
        out_specs=VMEM,
        compiler_params=pltpu.CompilerParams(vmem_limit_bytes=44 * 2**20),
        cost_estimate=pl.CostEstimate(
            flops=24 * rows * rows * HD,
            bytes_accessed=28 * rows * HD,
            transcendentals=6 * rows * rows,
        ),
        name="attend",
    )(usable, q, *pairs)


def update_kernel(
    step_ref, first_ref, returned_ref, residual_ref, incoming_ref, gate_ref, moving_ref, *parts
):
    gate = gate_ref[pl.ds(step_ref[0], 1), :]
    heads = parts[0].shape[0]
    first = first_ref[0] > 0
    for head in range(returned_ref.shape[0]):
        columns = slice(head * HD, (head + 1) * HD)
        updated = (
            residual_ref[0, :, columns].astype(jnp.float32)
            + gate[:, columns] * returned_ref[head].astype(jnp.float32)
        ).astype(jnp.bfloat16)
        moving_ref[0, :, columns] = jnp.where(first, incoming_ref[:, columns], updated)
        parts[head // heads][head % heads] = updated


def update(timesteps, first, returned, residual, incoming, gate_table):
    heads, tokens, _ = returned.shape
    part = jax.ShapeDtypeStruct((heads // 4, tokens, HD), jnp.bfloat16)
    moving, *parts = pl.pallas_call(
        update_kernel,
        out_shape=[jax.ShapeDtypeStruct(residual.shape, jnp.bfloat16)] + [part] * 4,
        in_specs=[SMEM, SMEM, VMEM, VMEM, VMEM, VMEM],
        out_specs=[VMEM] * 5,
        compiler_params=pltpu.CompilerParams(vmem_limit_bytes=16 * 2**20),
        name="update",
    )(timesteps, first, returned, residual, incoming, gate_table)
    return moving, parts


def finish_kernel(leads_ref, moved_ref, own_ref, *refs):
    *others, next_ref, leaving_ref = refs
    next_ref[...] = moved_ref[...]
    passed = sum(ref[...].astype(jnp.float32) for ref in others).astype(jnp.bfloat16)
    leaving_ref[...] = jnp.where(leads_ref[0] > 0, own_ref[...], passed)


def finish(leads, moved, own, others):
    return pl.pallas_call(
        finish_kernel,
        out_shape=[
            jax.ShapeDtypeStruct(moved.shape, moved.dtype),
            jax.ShapeDtypeStruct(own.shape, own.dtype),
        ],
        in_specs=[SMEM] + [VMEM] * (2 + len(others)),
        out_specs=[VMEM, VMEM],
        compiler_params=pltpu.CompilerParams(vmem_limit_bytes=16 * 2**20),
        name="finish",
    )(leads, moved, own, *others)


def spread(parts, axis):
    size = lax.axis_size(axis)
    step = len(parts)
    index = lax.axis_index(axis)
    firsts = [lax.ppermute(parts[a], axis, [(0, a * step)]) for a in range(1, step)]
    held = jnp.where(index == 0, parts[0], sum(firsts))
    seconds = [
        lax.ppermute(held[b], axis, [(a, a + b) for a in range(0, size, step)])
        for b in range(1, step)
    ]
    return held[0], seconds


def per_device(queries, keys, values, residual, incoming, gate_table, timesteps, positions):
    frame_index = lax.axis_index("frame")
    frames = lax.axis_size("frame")
    own = lax.all_to_all(
        pack(positions, keys, values), "head", split_axis=0, concat_axis=0, tiled=True
    )
    own, packed = lax.optimization_barrier((own, pack(positions, queries)))
    prior = shifted(own, "frame", 1)
    later = shifted(own, "frame", -1)
    q = lax.all_to_all(packed, "head", split_axis=0, concat_axis=0, tiled=True)
    pairs = (own, swapped(own), prior, swapped(prior), later, swapped(later))
    usable = jnp.stack([frame_index > 0, frame_index < frames - 1]).astype(jnp.int32)
    attention = attend(usable, q, pairs, query_rows=768)
    returned = lax.all_to_all(attention, "head", split_axis=0, concat_axis=0, tiled=True)
    first = (frame_index == 0).astype(jnp.int32)[None]
    moving, parts = update(timesteps, first, returned, residual, incoming, gate_table)
    next_queue = lax.ppermute(moving, "frame", [(i, (i - 1) % frames) for i in range(frames)])
    held, sent = spread(parts, "frame")
    leads = (frame_index % len(parts) == 0).astype(jnp.int32)[None]
    return tuple(finish(leads, next_queue, held, sent))


def solution(mesh):
    placed = (
        P("frame", ("head", "tok"), None),
        P("frame", ("head", "tok"), None),
        P("frame", ("head", "tok"), None),
        P("frame", ("head", "tok"), None),
        P(("head", "tok"), None),
        P(),
        P("frame"),
        P("frame"),
    )
    return jax.shard_map(
        per_device,
        mesh=mesh,
        in_specs=placed,
        out_specs=(P("frame", ("head", "tok"), None), P(("head", "tok"), "frame")),
        check_vma=False,
    )
```
